32 devices in a mesh: inner: 16 (over z, y, x), outer: 2 (over core).
Axes of the slice: x: 2, y: 2, z: 4, core: 2. Of those that a mesh axis runs over, the one named last changes fastest.
Arguments:
- feats_first: bfloat16 [2, 4096, 2048], P('outer', 'inner'), may hold values from -4 to 8
- feats_second: bfloat16 [2, 4096, 2048], P('outer', 'inner'), may hold values from -4 to 8
- expander: bfloat16 [2048, 1024], P('inner'), may hold values from -0.125 to 0.125
- tile_count: int32 [2, 16], replicated, may hold values from 64 to 256, as said below
- match_dev: int32 [2, 4096, 1], P('outer', 'inner'), may hold values from 0 to 15; in each aligned block of 256 rows (0 to 255, 256 to 511, ..., all dimensions but the last counted through in order) at most 48 rows name the same one
- match_tile: int32 [2, 4096], P('outer', 'inner'), may hold values from 0 to 255
Outputs:
- covariance: float32 [1024, 1024], P('inner')
- invariance: float32 [2, 4096], P('outer', 'inner')
The draws below stay inside these ranges and needn't reach their ends.
Inputs may be any that keep to these rules, and one draw needn't show every extreme that they name: `tile_count`: for every slide some device has all 256 tiles live; the others at least a quarter. `match_dev`: at most 48 tiles of one device name the same device.
All inputs are finite; a program needn't handle non-finite values.
Results may differ from the reference program's by a relative error of at most 0.00135.
Values may be sent and summed in bfloat16 or wider, within the bound.
A program may use at most 64 MiB of HBM per device.

```python
import math
import jax
import jax.numpy as jnp
import numpy as np

C = 2048
E = 1024
TILES = 256
SLIDES = 2
ROWS = 4096
CAP = 48
N_INNER = 16


def feature_draw(key, crop):
    shared_key = jax.random.fold_in(key, 101)
    offset_key, flip_key = jax.random.split(shared_key)
    crop_key = jax.random.fold_in(key, 211 + crop)
    base_key = jax.random.fold_in(crop_key, 0)
    positions = jnp.arange(ROWS, dtype=jnp.float32)[None, :, None]
    flipped = jax.random.bernoulli(flip_key, 0.5, (SLIDES, 1, 1))
    along = jnp.where(flipped, positions, ROWS - 1.0 - positions)
    row_ramp = 1.0 + 2.0 * along / (ROWS - 1.0)
    offsets = jnp.exp(jax.random.uniform(offset_key, (SLIDES, 1, C), jnp.float32, math.log(0.3), math.log(1.5)))
    noise_part = jax.random.normal(base_key, (SLIDES, ROWS, C), jnp.float32)
    values = jnp.clip(offsets * row_ramp + noise_part, -4.0, 8.0)
    return values.astype(jnp.bfloat16)


def draw_feats_first(key, part):
    return feature_draw(key, 0)


def draw_feats_second(key, part):
    return feature_draw(key, 1)


def draw_tile_count(key, part):
    first_key, second_key = jax.random.split(key)
    counts = jax.random.randint(first_key, (SLIDES, N_INNER), TILES // 4, TILES + 1)
    fullest = jax.random.randint(second_key, (SLIDES, 1), 0, N_INNER)
    column = jnp.arange(N_INNER, dtype=jnp.int32)[None, :]
    return jnp.where(column == fullest, TILES, counts).astype(jnp.int32)


def set_ends(values, stream_key, least, top_value):
    shape = values.shape
    index_at = [jax.random.randint(jax.random.fold_in(stream_key, axis), (), 0, shape[axis]) for axis in range(len(shape))]
    values = values.at[tuple(index_at)].set(least)
    longest = shape.index(max(shape))
    index_at[longest] = (index_at[longest] + 1) % shape[longest]
    return values.at[tuple(index_at)].set(top_value)


def shard_levels(rng, dims, cuts, smallest, top_value):
    gain, own = 1.0, jax.random.fold_in(rng, 6)
    for dim, shards_of in cuts:
        steps = jnp.exp(jax.random.uniform(jax.random.fold_in(own, dim), (shards_of,), jnp.float32, smallest / len(cuts), top_value / len(cuts)))
        gain = gain * jnp.repeat(steps, dims[dim] // shards_of).reshape([-1 if axis == dim else 1 for axis in range(len(dims))])
    return gain


def deal_out(rng, own, number, rows, count, top, limit, skew):
    order = jax.random.permutation(rng, count)
    packed, ordinary = portions_of(count, rows * top, limit, skew, True), portions_of(count, rows * top, limit, skew, False)
    places = jnp.arange(count)

    def named(tallies, offset_by):
        used = int((tallies > 0).sum())
        fixed = max(1, used // 4)
        passed = fixed + (places - fixed + offset_by * (used - fixed)) % max(1, count - fixed)
        return jnp.zeros((count,), jnp.int32).at[order[jnp.where(places < fixed, places, passed)]].set(jnp.asarray(tallies, jnp.int32))

    tallies = jnp.where(number % 4 == 0, named(packed, number // 4), named(ordinary, number - number // 4 - 1))
    mixed = jax.random.permutation(jax.random.fold_in(own, 3), count)
    giver, receiver = mixed[0:count // 2 * 2:2], mixed[1:count // 2 * 2:2]
    room = jnp.minimum(tallies[giver] - 1, limit - tallies[receiver]) // 2
    room = jnp.where((giver == order[0]) | (receiver == order[0]) | (tallies[receiver] == 0), 0, jnp.maximum(room, 0))
    passed = jax.random.randint(jax.random.fold_in(own, 4), (count // 2,), 0, 1 << 20) % (room + 1)
    tallies = tallies.at[giver].add(-passed).at[receiver].add(passed)
    labels = jnp.searchsorted(jnp.cumsum(tallies), jnp.arange(rows * top), side="right").astype(jnp.int32)
    grid = labels.reshape(top, rows).T
    grid = grid[jax.random.permutation(jax.random.fold_in(own, 1), rows)]
    offset_by = jax.random.randint(jax.random.fold_in(own, 2), (rows, 1), 0, top)
    return jnp.take_along_axis(grid, (jnp.arange(top)[None, :] + offset_by) % top, axis=1)


def portions_of(amount, total, most, skew, full):
    loads = [(1 << 20) // math.isqrt(grade ** skew) + 1 for grade in range(1, amount + 1)]
    largest = most if full else min(most, max(-(-total // amount), total * loads[0] // sum(loads)))
    least = 1 if total - largest >= amount - 1 else 0
    given, spare = [largest] + [least] * (amount - 1), total - largest - least * (amount - 1)
    while spare > 0:
        free = [i for i in range(1, amount) if given[i] < largest] or [i for i in range(1, amount) if given[i] < most]
        whole, budget = sum([loads[i] for i in free]), spare
        for i in free:
            addition = min(most - given[i], max(1, budget * loads[i] // whole), spare)
            given[i] = given[i] + addition
            spare = spare - addition
    return np.array(given)


def normal_values(own_key, extent, spread, reach, pieces=(), held_as=jnp.bfloat16):
    array = spread * jax.random.normal(own_key, extent, jnp.float32)
    if pieces:
        array = array * shard_levels(own_key, extent, pieces, -0.22, 0.18)
    return jnp.clip(array, -reach, reach).astype(held_as)


def setup_inputs(seed: int = 0) -> dict:
    key_list = jax.random.split(jax.random.key(seed), 7)
    feats_first = draw_feats_first(jax.random.fold_in(key_list[6], 71), 0)
    feats_second = draw_feats_second(jax.random.fold_in(key_list[6], 71), 0)
    expander = normal_values(key_list[2], (C, E), C ** -0.5, 0.125, ((0, 16),))
    tile_count = draw_tile_count(jax.random.fold_in(key_list[6], 71), 0)
    match_dev_keys = jax.random.split(jax.random.fold_in(key_list[4], 1), SLIDES * ROWS // TILES)
    match_dev_turns = jax.random.permutation(jax.random.fold_in(key_list[4], 3), SLIDES * ROWS // TILES)
    match_dev = jax.vmap(lambda own, number: deal_out(jax.random.fold_in(key_list[4], 2), own, number, TILES, N_INNER, 1, CAP, 2))(match_dev_keys, match_dev_turns).reshape((SLIDES, ROWS, 1))
    match_tile = set_ends(jax.random.randint(key_list[5], (SLIDES, ROWS), 0, TILES), jax.random.fold_in(key_list[5], 1), 0, TILES - 1).astype(jnp.int32)
    return dict(feats_first=feats_first, feats_second=feats_second, expander=expander, tile_count=tile_count, match_dev=match_dev, match_tile=match_tile)


def reference(feats_first, feats_second, expander, tile_count, match_dev, match_tile):
    gram = jnp.zeros((E, E), jnp.float32)
    column_sum = jnp.zeros((E,), jnp.float32)
    total = jnp.sum(tile_count).astype(jnp.float32)
    outputs = []
    positions = jnp.arange(ROWS, dtype=jnp.int32)
    owner = positions // TILES
    for slide in range(SLIDES):
        first_embed = jnp.dot(feats_first[slide], expander, preferred_element_type=jnp.float32).astype(jnp.bfloat16)
        second_embed = jnp.dot(feats_second[slide], expander, preferred_element_type=jnp.float32).astype(jnp.bfloat16)
        counts = tile_count[slide]
        live = (positions % TILES) < counts[owner]
        target_dev = match_dev[slide, :, 0]
        target_tile = match_tile[slide]
        partner = second_embed[(target_dev * TILES + target_tile).astype(jnp.int32)]
        valid = live & (target_tile < counts[target_dev])
        diff = first_embed.astype(jnp.float32) - partner.astype(jnp.float32)
        outputs.append(jnp.where(valid, jnp.mean(diff * diff, axis=-1), jnp.float32(0.0)))
        masked = jnp.where(live[:, None], first_embed, jnp.zeros_like(first_embed))
        column_sum = column_sum + jnp.sum(masked.astype(jnp.float32), axis=0)
        gram = gram + jnp.dot(masked.T, masked, preferred_element_type=jnp.float32)
    covariance = (gram - column_sum[:, None] * column_sum[None, :] / total) / (total - 1.0)
    return covariance, jnp.stack(outputs)
```

```python
import jax
import jax.numpy as jnp
from jax import lax
from jax.sharding import PartitionSpec as P


def shards(feats_first, feats_second, expander, tile_count, match_dev, match_tile):
    first_rows = feats_first[0]
    second_rows = feats_second[0]
    tile_rows = first_rows.shape[0]
    expand_width = expander.shape[1]
    group_size = lax.axis_size("inner")
    capacity = -(-max(2, 3 * tile_rows // group_size) // 16) * 16
    slots = group_size * capacity
    inner_pos = lax.axis_index("inner")
    outer_pos = lax.axis_index("outer")
    target_dev = match_dev[0, :, 0]
    target_tile = match_tile[0]
    row_index = jnp.arange(tile_rows, dtype=jnp.int32)
    same = (target_dev[:, None] == target_dev[None, :]) & (row_index[None, :] < row_index[:, None])
    slot_pos = jnp.sum(same.astype(jnp.int32), axis=1)
    slot = target_dev * capacity + slot_pos
    chosen = slot[:, None] == jnp.arange(slots, dtype=jnp.int32)[None, :]
    asked = jnp.sum(jnp.where(chosen, target_tile[:, None], 0), axis=0).reshape(group_size, capacity)
    wanted = lax.all_to_all(asked, "inner", split_axis=0, concat_axis=0, tiled=True).reshape(slots)
    piece = lax.all_gather(expander, "inner", axis=0, tiled=True)
    first_embed = jnp.dot(first_rows, piece, preferred_element_type=jnp.float32).astype(jnp.bfloat16)
    second_embed = jnp.dot(second_rows, piece, preferred_element_type=jnp.float32).astype(jnp.bfloat16)
    pick = (wanted[:, None] == row_index[None, :]).astype(jnp.bfloat16)
    send_rows = jnp.dot(pick, second_embed, preferred_element_type=jnp.float32).astype(jnp.bfloat16)
    recv_rows = lax.all_to_all(
        send_rows.reshape(group_size, capacity, expand_width), "inner", split_axis=0, concat_axis=0, tiled=True
    ).reshape(slots, expand_width)
    partner = jnp.dot(chosen.astype(jnp.bfloat16), recv_rows, preferred_element_type=jnp.float32)
    counts = lax.dynamic_index_in_dim(tile_count, outer_pos, 0, keepdims=False)
    own_count = lax.dynamic_index_in_dim(counts, inner_pos, 0, keepdims=False)
    live = row_index < own_count
    dest_count = jnp.sum(
        jnp.where(target_dev[:, None] == jnp.arange(group_size, dtype=jnp.int32)[None, :], counts[None, :], 0), axis=1
    )
    valid = live & (target_tile < dest_count)
    diff = first_embed.astype(jnp.float32) - partner
    invariance = jnp.where(valid, jnp.mean(diff * diff, axis=-1), jnp.float32(0.0))
    masked = jnp.where(live[:, None], first_embed, jnp.zeros_like(first_embed))
    column_total = lax.psum(jnp.sum(masked.astype(jnp.float32), axis=0), ("inner", "outer"))
    total = jnp.sum(tile_count).astype(jnp.float32)
    share_rows = expand_width // group_size
    local_share = lax.psum_scatter(
        lax.dot_general(masked, masked, (((0,), (0,)), ((), ())), preferred_element_type=jnp.float32),
        "inner",
        scatter_dimension=0,
        tiled=True,
    )
    gram_share = lax.psum(local_share, "outer")
    own_sums = lax.dynamic_slice_in_dim(column_total, inner_pos * share_rows, share_rows, 0)
    covariance = (gram_share - own_sums[:, None] * column_total[None, :] / total) / (total - 1.0)
    return (covariance, invariance[None, :])


def solution(mesh):
    return jax.shard_map(
        shards,
        mesh=mesh,
        in_specs=(
            P("outer", "inner", None),
            P("outer", "inner", None),
            P("inner", None),
            P(),
            P("outer", "inner", None),
            P("outer", "inner"),
        ),
        out_specs=(P("inner", None), P("outer", "inner")),
        check_vma=False,
    )
```

```python
import functools

import jax
import jax.numpy as jnp
from jax import lax
from jax.experimental import pallas as pl
from jax.experimental.pallas import tpu as pltpu
from jax.sharding import PartitionSpec as P

MESH = pl.DeviceIdType.MESH


def minor_size(n):
    return 4 if n % 4 == 0 and n > 4 else 1


def greet(n, m):
    me, core = lax.axis_index("inner"), lax.axis_index("outer")
    barrier = pltpu.get_barrier_semaphore()

    def inner(k, c):
        pl.semaphore_signal(barrier, inc=1, device_id={"inner": lax.rem(me + k, n)}, device_id_type=MESH)
        return c

    lax.fori_loop(1, n, inner, 0)
    for t in range(1, m):
        pl.semaphore_signal(barrier, inc=1, device_id={"outer": lax.rem(core + t, m)}, device_id_type=MESH)
    pl.semaphore_wait(barrier, n - 1 + m - 1)


def remote(src, dst, sems, at, device):
    return pltpu.make_async_remote_copy(
        src_ref=src,
        dst_ref=dst,
        send_sem=sems[0].at[at],
        recv_sem=sems[1].at[at],
        device_id=device,
        device_id_type=MESH,
    )


def each(low, high, body):
    def step(k, c):
        body(k)
        return c

    lax.fori_loop(low, high, step, 0)


def gather_kernel(n, m, w, ask, full, got, zs, zr, ps, pr, os, orr, qs, qr):
    me, core = lax.axis_index("inner"), lax.axis_index("outer")
    minor = minor_size(n)
    major = n // minor
    a, b = me // minor, lax.rem(me, minor)
    part = w.shape[1] // m

    def cols(t):
        return pl.ds(pl.multiple_of(t * part, 128), part)

    mine = cols(core)
    greet(n, m)

    def z_copy(k, index):
        peer = lax.rem(a + k, major) * minor + b
        return remote(w.at[:, mine], full.at[index, :, mine], (zs, zr), k, {"inner": peer})

    def p_copy(k, j, index):
        peer = a * minor + lax.rem(b + j, minor)
        source = w.at[:, mine] if k is None else full.at[index, :, mine]
        at = j if k is None else k * minor + j
        return remote(source, full.at[index, :, mine], (ps, pr), at, {"inner": peer})

    def o_copy(t, index, at, lanes):
        block = full.at[index, :, lanes]
        return remote(block, block, (os, orr), t * n + at, {"outer": lax.rem(core + t, m)})

    def q_copy(k, index):
        return remote(ask.at[lax.rem(me + k, n)], got.at[index], (qs, qr), k, {"inner": lax.rem(me + k, n)})

    def block_of(k, j):
        return lax.rem(a - k + major, major) * minor + lax.rem(b - j + minor, minor)

    each(1, major, lambda k: z_copy(k, me).start())
    for j in range(1, minor):
        p_copy(None, j, me).start()
    each(1, n, lambda k: q_copy(k, me).start())
    full[me] = w[...]
    got[me] = ask[me]

    def relay(k):
        index = block_of(k, 0)
        z_copy(k, index).wait_recv()
        for j in range(1, minor):
            p_copy(k, j, index).start()
        for t in range(1, m):
            o_copy(t, index, k * minor, mine).start()

    each(1, major, relay)

    def share(k):
        for j in range(1, minor):
            index = block_of(k, j)
            p_copy(k, j, index).wait_recv()
            for t in range(1, m):
                o_copy(t, index, k * minor + j, mine).start()

    each(0, major, share)

    def settle(k):
        for j in range(minor):
            for t in range(1, m):
                copy = o_copy(t, block_of(k, j), k * minor + j, cols(lax.rem(core - t + m, m)))
                if j == 0:

                    @pl.when(k > 0)
                    def _():
                        copy.wait_recv()
                        copy.wait_send()
                else:
                    copy.wait_recv()
                    copy.wait_send()
            if j > 0:
                p_copy(k, j, block_of(k, 0)).wait_send()

    each(0, major, settle)
    each(1, major, lambda k: z_copy(k, me).wait_send())

    def questions(k):
        copy = q_copy(k, lax.rem(me - k + n, n))
        copy.wait_recv()
        copy.wait_send()

    each(1, n, questions)


def gather(expander, asked, n, m):
    depth, width = expander.shape
    dma = pltpu.SemaphoreType.DMA
    minor = minor_size(n)
    vmem = pl.BlockSpec(memory_space=pltpu.VMEM)
    return pl.pallas_call(
        functools.partial(gather_kernel, n, m),
        out_shape=(
            jax.ShapeDtypeStruct((n, depth, width), expander.dtype),
            jax.ShapeDtypeStruct(asked.shape, asked.dtype),
        ),
        in_specs=[vmem] * 2,
        out_specs=(vmem, vmem),
        scratch_shapes=[
            dma((n // minor,)), dma((n // minor,)), dma((n,)), dma((n,)), dma((m * n,)), dma((m * n,)), dma((n,)), dma((n,)),
        ],
        compiler_params=pltpu.CompilerParams(collective_id=0, has_side_effects=True, vmem_limit_bytes=40 << 20),
        name="gather",
    )(expander, asked)


def exchange_kernel(n, m, rows, gram, sums, got, out, total, landed, half, plane, line, last,
                    s_core, s_all, rs, rr, os, orr, ps, pr, zs, zr, fs, fr, cs, cr, ss, sr):
    me, core = lax.axis_index("inner"), lax.axis_index("outer")
    minor = minor_size(n)
    major = n // minor
    a, b = me // minor, lax.rem(me, minor)
    part = out.shape[1] // m

    def cols(t):
        return pl.ds(pl.multiple_of(t * part, 128), part)

    mine = cols(core)
    greet(n, m)

    def o_copy(t):
        peer = lax.rem(core + t, m)
        return remote(gram.at[:, :, :, cols(peer)], landed.at[t], (os, orr), t, {"outer": peer})

    def c_copy(t, index):
        return remote(sums, s_core.at[index], (cs, cr), t, {"outer": lax.rem(core + t, m)})

    def r_copy(k, index):
        peer = lax.rem(me + k, n)
        return remote(rows.at[peer], got.at[index], (rs, rr), k, {"inner": peer})

    def p_copy(j):
        other = lax.rem(b + j, minor)
        return remote(half.at[:, other], plane.at[j], (ps, pr), j, {"inner": a * minor + other})

    def z_copy(k):
        other = lax.rem(a + k, major)
        return remote(line.at[other], last.at[k], (zs, zr), k, {"inner": other * minor + b})

    def s_copy(k, index):
        return remote(s_all.at[index], s_all.at[index], (ss, sr), k, {"inner": lax.rem(me + k, n)})

    def f_copy(t, lanes):
        return remote(out.at[:, lanes], out.at[:, lanes], (fs, fr), t, {"outer": lax.rem(core + t, m)})

    for t in range(1, m):
        c_copy(t, core).start()
        o_copy(t).start()
    each(1, n, lambda k: r_copy(k, me).start())
    got[me] = rows[me]
    s_core[core] = sums[...]
    for t in range(1, m):
        c_copy(t, lax.rem(core - t + m, m)).wait_recv()
    s_all[me] = functools.reduce(lambda x, y: x + y, [s_core[t] for t in range(m)])
    each(1, n, lambda k: s_copy(k, me).start())
    for t in range(1, m):
        o_copy(t).wait_recv()

    def add_cores(i):
        x, y = i // minor, lax.rem(i, minor)
        value = gram[x, y, :, mine]
        for t in range(1, m):
            value = value + landed[t, x, y]
        half[x, y] = value

    each(0, n, add_cores)
    for j in range(1, minor):
        p_copy(j).start()
    for j in range(1, minor):
        p_copy(j).wait_recv()

    def add_plane(x):
        value = half[x, b]
        for j in range(1, minor):
            value = value + plane[j, x]
        line[x] = value

    each(0, major, add_plane)
    each(1, major, lambda k: z_copy(k).start())
    each(1, major, lambda k: z_copy(k).wait_recv())
    value = line[a]
    for k in range(1, major):
        value = value + last[k]
    out[:, mine] = value
    for t in range(1, m):
        f_copy(t, mine).start()
    each(1, n, lambda k: s_copy(k, lax.rem(me - k + n, n)).wait_recv())
    value = s_all[0]
    for k in range(1, n):
        value = value + s_all[k]
    total[...] = value

    def settle(k):
        r_copy(k, lax.rem(me - k + n, n)).wait_recv()
        r_copy(k, me).wait_send()
        s_copy(k, me).wait_send()

    each(1, n, settle)
    for t in range(1, m):
        f_copy(t, cols(lax.rem(core - t + m, m))).wait_recv()
        f_copy(t, mine).wait_send()
        o_copy(t).wait_send()
        c_copy(t, core).wait_send()
    for j in range(1, minor):
        p_copy(j).wait_send()
    each(1, major, lambda k: z_copy(k).wait_send())


def exchange(rows, gram, sums, n, m):
    width = gram.shape[1]
    share, part = width // n, width // m
    minor = minor_size(n)
    major = n // minor
    dma = pltpu.SemaphoreType.DMA
    vmem = pl.BlockSpec(memory_space=pltpu.VMEM)
    f32 = jnp.float32
    pairs = [n, m, minor, major, m, m, n]
    return pl.pallas_call(
        functools.partial(exchange_kernel, n, m),
        out_shape=(
            jax.ShapeDtypeStruct(rows.shape, rows.dtype),
            jax.ShapeDtypeStruct((share, width), f32),
            jax.ShapeDtypeStruct((1, width), f32),
        ),
        in_specs=[vmem] * 3,
        out_specs=(vmem,) * 3,
        scratch_shapes=[
            pltpu.VMEM((m, major, minor, share, part), f32),
            pltpu.VMEM((major, minor, share, part), f32),
            pltpu.VMEM((minor, major, share, part), f32),
            pltpu.VMEM((major, share, part), f32),
            pltpu.VMEM((major, share, part), f32),
            pltpu.VMEM((m, 1, width), f32),
            pltpu.VMEM((n, 1, width), f32),
        ]
        + [dma((size,)) for size in pairs for _ in range(2)],
        compiler_params=pltpu.CompilerParams(collective_id=1, has_side_effects=True, vmem_limit_bytes=40 << 20),
        name="exchange",
    )(rows, gram.reshape(major, minor, share, width), sums)


def shards(feats_first, feats_second, expander, tile_count, match_dev, match_tile):
    first_rows = feats_first[0]
    second_rows = feats_second[0]
    tile_rows = first_rows.shape[0]
    expand_width = expander.shape[1]
    group_size = lax.axis_size("inner")
    capacity = -(-max(2, 3 * tile_rows // group_size) // 16) * 16
    slots = group_size * capacity
    inner_pos = lax.axis_index("inner")
    outer_pos = lax.axis_index("outer")
    target_dev = match_dev[0, :, 0]
    target_tile = match_tile[0]
    row_index = jnp.arange(tile_rows, dtype=jnp.int32)
    same = (target_dev[:, None] == target_dev[None, :]) & (row_index[None, :] < row_index[:, None])
    slot_pos = jnp.sum(same.astype(jnp.int32), axis=1)
    slot = target_dev * capacity + slot_pos
    chosen = slot[:, None] == jnp.arange(slots, dtype=jnp.int32)[None, :]
    padded = -(-capacity // 128) * 128
    asked = jnp.sum(jnp.where(chosen, target_tile[:, None], 0), axis=0).reshape(group_size, 1, capacity)
    asked = jnp.pad(asked, ((0, 0), (0, 0), (0, padded - capacity)))
    piece, wanted = gather(expander, asked, group_size, lax.axis_size("outer"))
    piece = piece.reshape(-1, expand_width)
    wanted = wanted[:, 0, :capacity].reshape(slots)
    first_embed = jnp.dot(first_rows, piece, preferred_element_type=jnp.float32).astype(jnp.bfloat16)
    second_embed = jnp.dot(second_rows, piece, preferred_element_type=jnp.float32).astype(jnp.bfloat16)
    pick = (wanted[:, None] == row_index[None, :]).astype(jnp.bfloat16)
    send_rows = jnp.dot(pick, second_embed, preferred_element_type=jnp.float32).astype(jnp.bfloat16)
    counts = lax.dynamic_index_in_dim(tile_count, outer_pos, 0, keepdims=False)
    own_count = lax.dynamic_index_in_dim(counts, inner_pos, 0, keepdims=False)
    live = row_index < own_count
    masked = jnp.where(live[:, None], first_embed, jnp.zeros_like(first_embed))
    gram = lax.dot_general(masked, masked, (((0,), (0,)), ((), ())), preferred_element_type=jnp.float32)
    recv_rows, gram_share, column_total = exchange(
        send_rows.reshape(group_size, capacity, expand_width),
        gram,
        jnp.sum(masked.astype(jnp.float32), axis=0, keepdims=True),
        group_size,
        lax.axis_size("outer"),
    )
    recv_rows = recv_rows.reshape(slots, expand_width)
    column_total = column_total[0]
    partner = jnp.dot(chosen.astype(jnp.bfloat16), recv_rows, preferred_element_type=jnp.float32)
    dest_count = jnp.sum(
        jnp.where(target_dev[:, None] == jnp.arange(group_size, dtype=jnp.int32)[None, :], counts[None, :], 0), axis=1
    )
    valid = live & (target_tile < dest_count)
    diff = first_embed.astype(jnp.float32) - partner
    invariance = jnp.where(valid, jnp.mean(diff * diff, axis=-1), jnp.float32(0.0))
    total = jnp.sum(tile_count).astype(jnp.float32)
    share_rows = expand_width // group_size
    own_sums = lax.dynamic_slice_in_dim(column_total, inner_pos * share_rows, share_rows, 0)
    covariance = (gram_share - own_sums[:, None] * column_total[None, :] / total) / (total - 1.0)
    return (covariance, invariance[None, :])


def solution(mesh):
    return jax.shard_map(
        shards,
        mesh=mesh,
        in_specs=(
            P("outer", "inner", None),
            P("outer", "inner", None),
            P("inner", None),
            P(),
            P("outer", "inner", None),
            P("outer", "inner"),
        ),
        out_specs=(P("inner", None), P("outer", "inner")),
        check_vma=False,
    )
```

```python
import functools

import jax
import jax.numpy as jnp
from jax import lax
from jax.experimental import pallas as pl
from jax.experimental.pallas import tpu as pltpu
from jax.sharding import PartitionSpec as P

MESH = pl.DeviceIdType.MESH


def minor_size(n):
    return 4 if n % 4 == 0 and n > 4 else 1


def greet(n, m):
    me, core = lax.axis_index("inner"), lax.axis_index("outer")
    barrier = pltpu.get_barrier_semaphore()

    def inner(k, c):
        pl.semaphore_signal(barrier, inc=1, device_id={"inner": lax.rem(me + k, n)}, device_id_type=MESH)
        return c

    lax.fori_loop(1, n, inner, 0)
    for t in range(1, m):
        pl.semaphore_signal(barrier, inc=1, device_id={"outer": lax.rem(core + t, m)}, device_id_type=MESH)
    pl.semaphore_wait(barrier, n - 1 + m - 1)


def remote(src, dst, sems, at, device):
    return pltpu.make_async_remote_copy(
        src_ref=src,
        dst_ref=dst,
        send_sem=sems[0].at[at],
        recv_sem=sems[1].at[at],
        device_id=device,
        device_id_type=MESH,
    )


def each(low, high, body):
    def step(k, c):
        body(k)
        return c

    lax.fori_loop(low, high, step, 0)


def gather_kernel(n, m, w, ask, first, second, got, first_embed, second_embed, full, feats, acc,
                  zs, zr, ps, pr, os, orr, qs, qr, loads):
    me, core = lax.axis_index("inner"), lax.axis_index("outer")
    minor = minor_size(n)
    major = n // minor
    a, b = me // minor, lax.rem(me, minor)
    depth, width = w.shape
    part = width // m
    chunk = minor * depth
    lanes = min(width, 256)

    def cols(t):
        return pl.ds(pl.multiple_of(t * part, 128), part)

    def block(x, y, columns):
        return full.at[x, pl.ds(pl.multiple_of(y * depth, depth), depth), columns]

    mine = cols(core)
    greet(n, m)

    def z_copy(k, x):
        peer = lax.rem(a + k, major) * minor + b
        return remote(w.at[:, mine], block(x, b, mine), (zs, zr), k, {"inner": peer})

    def p_copy(k, j, x, y):
        peer = a * minor + lax.rem(b + j, minor)
        source = w.at[:, mine] if k is None else block(x, y, mine)
        at = j if k is None else k * minor + j
        return remote(source, block(x, y, mine), (ps, pr), at, {"inner": peer})

    def o_copy(t, x, y, at, columns):
        return remote(
            block(x, y, columns), block(x, y, columns), (os, orr), t * n + at, {"outer": lax.rem(core + t, m)}
        )

    def q_copy(k, index):
        return remote(ask.at[lax.rem(me + k, n)], got.at[index], (qs, qr), k, {"inner": lax.rem(me + k, n)})

    def plane(k):
        return lax.rem(a - k + major, major)

    def column(j):
        return lax.rem(b - j + minor, minor)

    each(1, major, lambda k: z_copy(k, a).start())
    for j in range(1, minor):
        p_copy(None, j, a, b).start()
    fetch = [pltpu.make_async_copy(ref, feats.at[i], loads.at[i]) for i, ref in enumerate((first, second))]
    for copy in fetch:
        copy.start()
    each(1, n, lambda k: q_copy(k, me).start())
    full[a, pl.ds(pl.multiple_of(b * depth, depth), depth), :] = w[...]
    got[me] = ask[me]
    acc[...] = jnp.zeros_like(acc)

    def relay(k):
        x = plane(k)
        z_copy(k, x).wait_recv()
        for j in range(1, minor):
            p_copy(k, j, x, b).start()
        for t in range(1, m):
            o_copy(t, x, b, k * minor, mine).start()

    each(1, major, relay)

    def share(k):
        for j in range(1, minor):
            p_copy(k, j, plane(k), column(j)).wait_recv()
            for t in range(1, m):
                o_copy(t, plane(k), column(j), k * minor + j, mine).start()

    def multiply(k):
        x = plane(k)
        for j in range(minor):
            for t in range(1, m):
                copy = o_copy(t, x, column(j), k * minor + j, cols(lax.rem(core - t + m, m)))
                if j == 0:

                    @pl.when(k > 0)
                    def _():
                        copy.wait_recv()
                else:
                    copy.wait_recv()
        deep = pl.ds(pl.multiple_of(x * chunk, 128), chunk)

        def columns(c):
            at = pl.ds(pl.multiple_of(c * lanes, lanes), lanes)
            for i in range(2):
                acc[i, :, at] += jnp.dot(feats[i, :, deep], full[x, :, at], preferred_element_type=jnp.float32)

        each(0, width // lanes, columns)

    share(0)
    for copy in fetch:
        copy.wait()

    def steps(k):
        share(k)
        multiply(k - 1)

    each(1, major, steps)
    multiply(major - 1)
    first_embed[...] = acc[0].astype(first_embed.dtype)
    second_embed[...] = acc[1].astype(second_embed.dtype)

    def settle(k):
        for j in range(minor):
            for t in range(1, m):
                copy = o_copy(t, plane(k), column(j), k * minor + j, mine)
                if j == 0:

                    @pl.when(k > 0)
                    def _():
                        copy.wait_send()
                else:
                    copy.wait_send()
            if j > 0:
                p_copy(k, j, plane(k), b).wait_send()

    each(0, major, settle)
    each(1, major, lambda k: z_copy(k, a).wait_send())

    def questions(k):
        copy = q_copy(k, lax.rem(me - k + n, n))
        copy.wait_recv()
        copy.wait_send()

    each(1, n, questions)


def gather(expander, asked, first, second, n, m):
    depth, width = expander.shape
    rows, channels = first.shape
    dma = pltpu.SemaphoreType.DMA
    minor = minor_size(n)
    major = n // minor
    vmem = pl.BlockSpec(memory_space=pltpu.VMEM)
    embed = jax.ShapeDtypeStruct((rows, width), jnp.bfloat16)
    return pl.pallas_call(
        functools.partial(gather_kernel, n, m),
        out_shape=(jax.ShapeDtypeStruct(asked.shape, asked.dtype), embed, embed),
        in_specs=[vmem] * 2 + [pl.BlockSpec(memory_space=pl.ANY)] * 2,
        out_specs=(vmem,) * 3,
        scratch_shapes=[
            pltpu.VMEM((major, minor * depth, width), expander.dtype),
            pltpu.VMEM((2, rows, channels), first.dtype),
            pltpu.VMEM((2, rows, width), jnp.float32),
        ]
        + [dma((size,)) for size in (major, n, m * n, n) for _ in range(2)]
        + [dma((2,))],
        compiler_params=pltpu.CompilerParams(collective_id=0, has_side_effects=True, vmem_limit_bytes=40 << 20),
        name="gather",
    )(expander, asked, first, second)


def exchange_kernel(n, m, rows, gram, sums, got, out, s_all, landed, half, plane, line, last,
                    s_core, rs, rr, os, orr, ps, pr, zs, zr, fs, fr, cs, cr, ss, sr):
    me, core = lax.axis_index("inner"), lax.axis_index("outer")
    minor = minor_size(n)
    major = n // minor
    a, b = me // minor, lax.rem(me, minor)
    part = out.shape[1] // m

    def cols(t):
        return pl.ds(pl.multiple_of(t * part, 128), part)

    mine = cols(core)
    greet(n, m)

    def o_copy(t):
        peer = lax.rem(core + t, m)
        return remote(gram.at[:, :, :, cols(peer)], landed.at[t], (os, orr), t, {"outer": peer})

    def c_copy(t, index):
        return remote(sums, s_core.at[index], (cs, cr), t, {"outer": lax.rem(core + t, m)})

    def r_copy(k, index):
        peer = lax.rem(me + k, n)
        return remote(rows.at[peer], got.at[index], (rs, rr), k, {"inner": peer})

    def p_copy(j):
        other = lax.rem(b + j, minor)
        return remote(half.at[:, other], plane.at[j], (ps, pr), j, {"inner": a * minor + other})

    def z_copy(k):
        other = lax.rem(a + k, major)
        return remote(line.at[other], last.at[k], (zs, zr), k, {"inner": other * minor + b})

    def s_copy(k, index):
        return remote(s_core, s_all.at[index], (ss, sr), k, {"inner": lax.rem(me + k, n)})

    def f_copy(t, lanes):
        return remote(out.at[:, lanes], out.at[:, lanes], (fs, fr), t, {"outer": lax.rem(core + t, m)})

    for t in range(1, m):
        c_copy(t, core).start()
        o_copy(t).start()
    each(1, n, lambda k: r_copy(k, me).start())
    got[me] = rows[me]
    s_core[core] = sums[...]
    for t in range(1, m):
        c_copy(t, lax.rem(core - t + m, m)).wait_recv()
    s_all[me] = s_core[...]
    each(1, n, lambda k: s_copy(k, me).start())
    for t in range(1, m):
        o_copy(t).wait_recv()

    def over_cores(x, y):
        value = gram[x, y, :, mine]
        for t in range(1, m):
            value = value + landed[t, x, y]
        return value

    def add_cores(i):
        x, y = i // minor, lax.rem(i, minor)
        half[x, y] = over_cores(x, y).astype(half.dtype)

    each(0, n, add_cores)
    for j in range(1, minor):
        p_copy(j).start()
    for j in range(1, minor):
        p_copy(j).wait_recv()

    def add_plane(x):
        value = over_cores(x, b)
        for j in range(1, minor):
            value = value + plane[j, x].astype(jnp.float32)
        line[x] = value

    each(0, major, add_plane)
    each(1, major, lambda k: z_copy(k).start())
    each(1, major, lambda k: z_copy(k).wait_recv())
    value = line[a]
    for k in range(1, major):
        value = value + last[k]
    out[:, mine] = value
    for t in range(1, m):
        f_copy(t, mine).start()
    each(1, n, lambda k: s_copy(k, lax.rem(me - k + n, n)).wait_recv())

    def settle(k):
        r_copy(k, lax.rem(me - k + n, n)).wait_recv()
        r_copy(k, me).wait_send()
        s_copy(k, me).wait_send()

    each(1, n, settle)
    for t in range(1, m):
        f_copy(t, cols(lax.rem(core - t + m, m))).wait_recv()
        f_copy(t, mine).wait_send()
        o_copy(t).wait_send()
        c_copy(t, core).wait_send()
    for j in range(1, minor):
        p_copy(j).wait_send()
    each(1, major, lambda k: z_copy(k).wait_send())


def exchange(rows, gram, sums, n, m):
    width = gram.shape[1]
    share, part = width // n, width // m
    minor = minor_size(n)
    major = n // minor
    dma = pltpu.SemaphoreType.DMA
    vmem = pl.BlockSpec(memory_space=pltpu.VMEM)
    f32 = jnp.float32
    pairs = [n, m, minor, major, m, m, n]
    return pl.pallas_call(
        functools.partial(exchange_kernel, n, m),
        out_shape=(
            jax.ShapeDtypeStruct(rows.shape, rows.dtype),
            jax.ShapeDtypeStruct((share, width), f32),
            jax.ShapeDtypeStruct((n, m, 1, width), f32),
        ),
        in_specs=[vmem] * 3,
        out_specs=(vmem,) * 3,
        scratch_shapes=[
            pltpu.VMEM((m, major, minor, share, part), f32),
            pltpu.VMEM((major, minor, share, part), jnp.bfloat16),
            pltpu.VMEM((minor, major, share, part), jnp.bfloat16),
            pltpu.VMEM((major, share, part), f32),
            pltpu.VMEM((major, share, part), f32),
            pltpu.VMEM((m, 1, width), f32),
        ]
        + [dma((size,)) for size in pairs for _ in range(2)],
        compiler_params=pltpu.CompilerParams(collective_id=1, has_side_effects=True, vmem_limit_bytes=40 << 20),
        name="exchange",
    )(rows, gram.reshape(major, minor, share, width), sums)


def shards(feats_first, feats_second, expander, tile_count, match_dev, match_tile):
    first_rows = feats_first[0]
    second_rows = feats_second[0]
    tile_rows = first_rows.shape[0]
    expand_width = expander.shape[1]
    group_size = lax.axis_size("inner")
    capacity = -(-max(2, 3 * tile_rows // group_size) // 16) * 16
    slots = group_size * capacity
    inner_pos = lax.axis_index("inner")
    outer_pos = lax.axis_index("outer")
    target_dev = match_dev[0, :, 0]
    target_tile = match_tile[0]
    row_index = jnp.arange(tile_rows, dtype=jnp.int32)
    same = (target_dev[:, None] == target_dev[None, :]) & (row_index[None, :] < row_index[:, None])
    slot_pos = jnp.sum(same.astype(jnp.int32), axis=1)
    slot = target_dev * capacity + slot_pos
    chosen = slot[:, None] == jnp.arange(slots, dtype=jnp.int32)[None, :]
    padded = -(-capacity // 128) * 128
    asked = jnp.sum(jnp.where(chosen, target_tile[:, None], 0), axis=0).reshape(group_size, 1, capacity)
    asked = jnp.pad(asked, ((0, 0), (0, 0), (0, padded - capacity)))
    wanted, first_embed, second_embed = gather(
        expander, asked, first_rows, second_rows, group_size, lax.axis_size("outer")
    )
    wanted = wanted[:, 0, :capacity].reshape(slots)
    pick = (wanted[:, None] == row_index[None, :]).astype(jnp.bfloat16)
    send_rows = jnp.dot(pick, second_embed, preferred_element_type=jnp.float32).astype(jnp.bfloat16)
    counts = lax.dynamic_index_in_dim(tile_count, outer_pos, 0, keepdims=False)
    own_count = lax.dynamic_index_in_dim(counts, inner_pos, 0, keepdims=False)
    live = row_index < own_count
    masked = jnp.where(live[:, None], first_embed, jnp.zeros_like(first_embed))
    gram = lax.dot_general(masked, masked, (((0,), (0,)), ((), ())), preferred_element_type=jnp.float32)
    sums = jnp.sum(masked.astype(jnp.float32), axis=0)
    gram = gram - sums[:, None] * (sums / own_count.astype(jnp.float32))[None, :]
    recv_rows, gram_share, all_sums = exchange(
        send_rows.reshape(group_size, capacity, expand_width),
        gram,
        sums[None, :],
        group_size,
        lax.axis_size("outer"),
    )
    recv_rows = recv_rows.reshape(slots, expand_width)
    partner = jnp.dot(chosen.astype(jnp.bfloat16), recv_rows, preferred_element_type=jnp.float32)
    dest_count = jnp.sum(
        jnp.where(target_dev[:, None] == jnp.arange(group_size, dtype=jnp.int32)[None, :], counts[None, :], 0), axis=1
    )
    valid = live & (target_tile < dest_count)
    diff = first_embed.astype(jnp.float32) - partner
    invariance = jnp.where(valid, jnp.mean(diff * diff, axis=-1), jnp.float32(0.0))
    total = jnp.sum(tile_count).astype(jnp.float32)
    share_rows = expand_width // group_size
    all_sums = all_sums.reshape(-1, expand_width)
    column_total = jnp.sum(all_sums, axis=0)
    own_part = lax.dynamic_slice_in_dim(all_sums, inner_pos * share_rows, share_rows, 1)
    own_sums = jnp.sum(own_part, axis=0)
    weights = 1.0 / tile_count.T.reshape(-1).astype(jnp.float32)
    between = lax.dot_general(
        own_part * weights[:, None], all_sums, (((0,), (0,)), ((), ())), precision=lax.Precision.HIGHEST
    )
    covariance = (gram_share + between - own_sums[:, None] * column_total[None, :] / total) / (total - 1.0)
    return (covariance, invariance[None, :])


def solution(mesh):
    return jax.shard_map(
        shards,
        mesh=mesh,
        in_specs=(
            P("outer", "inner", None),
            P("outer", "inner", None),
            P("inner", None),
            P(),
            P("outer", "inner", None),
            P("outer", "inner"),
        ),
        out_specs=(P("inner", None), P("outer", "inner")),
        check_vma=False,
    )
```

```python
import functools

import jax
import jax.numpy as jnp
from jax import lax
from jax.experimental import pallas as pl
from jax.experimental.pallas import tpu as pltpu
from jax.sharding import PartitionSpec as P

MESH = pl.DeviceIdType.MESH


def minor_size(n):
    return 4 if n % 4 == 0 and n > 4 else 1


def greet(n, m):
    me, core = lax.axis_index("inner"), lax.axis_index("outer")
    barrier = pltpu.get_barrier_semaphore()

    def inner(k, c):
        pl.semaphore_signal(barrier, inc=1, device_id={"inner": lax.rem(me + k, n)}, device_id_type=MESH)
        return c

    lax.fori_loop(1, n, inner, 0)
    for t in range(1, m):
        pl.semaphore_signal(barrier, inc=1, device_id={"outer": lax.rem(core + t, m)}, device_id_type=MESH)
    pl.semaphore_wait(barrier, n - 1 + m - 1)


def remote(src, dst, sems, at, device):
    return pltpu.make_async_remote_copy(
        src_ref=src,
        dst_ref=dst,
        send_sem=sems[0].at[at],
        recv_sem=sems[1].at[at],
        device_id=device,
        device_id_type=MESH,
    )


def each(low, high, body):
    def step(k, c):
        body(k)
        return c

    lax.fori_loop(low, high, step, 0)


def gather_part(n, m, w, ask, first, second, got, first_embed, second_embed, full, feats, acc,
                zs, zr, ps, pr, os, orr, qs, qr, loads):
    me, core = lax.axis_index("inner"), lax.axis_index("outer")
    minor = minor_size(n)
    major = n // minor
    a, b = me // minor, lax.rem(me, minor)
    depth, width = w.shape
    part = width // m
    chunk = minor * depth
    lanes = min(width, 256)

    def cols(t):
        return pl.ds(pl.multiple_of(t * part, 128), part)

    def block(x, y, columns):
        return full.at[x, pl.ds(pl.multiple_of(y * depth, depth), depth), columns]

    mine = cols(core)
    greet(n, m)

    def z_copy(k, x):
        peer = lax.rem(a + k, major) * minor + b
        return remote(w.at[:, mine], block(x, b, mine), (zs, zr), k, {"inner": peer})

    def p_copy(k, j, x, y):
        peer = a * minor + lax.rem(b + j, minor)
        source = w.at[:, mine] if k is None else block(x, y, mine)
        at = j if k is None else k * minor + j
        return remote(source, block(x, y, mine), (ps, pr), at, {"inner": peer})

    def o_copy(t, x, y, at, columns):
        return remote(
            block(x, y, columns), block(x, y, columns), (os, orr), t * n + at, {"outer": lax.rem(core + t, m)}
        )

    def q_copy(k, index):
        return remote(ask.at[lax.rem(me + k, n)], got.at[index], (qs, qr), k, {"inner": lax.rem(me + k, n)})

    def plane(k):
        return lax.rem(a - k + major, major)

    def column(j):
        return lax.rem(b - j + minor, minor)

    each(1, major, lambda k: z_copy(k, a).start())
    for j in range(1, minor):
        p_copy(None, j, a, b).start()
    fetch = [pltpu.make_async_copy(ref, feats.at[i], loads.at[i]) for i, ref in enumerate((first, second))]
    for copy in fetch:
        copy.start()
    each(1, n, lambda k: q_copy(k, me).start())
    full[a, pl.ds(pl.multiple_of(b * depth, depth), depth), :] = w[...]
    got[me] = ask[me]
    acc[...] = jnp.zeros_like(acc)

    def relay(k):
        x = plane(k)
        z_copy(k, x).wait_recv()
        for j in range(1, minor):
            p_copy(k, j, x, b).start()
        for t in range(1, m):
            o_copy(t, x, b, k * minor, mine).start()

    each(1, major, relay)

    def share(k):
        for j in range(1, minor):
            p_copy(k, j, plane(k), column(j)).wait_recv()
            for t in range(1, m):
                o_copy(t, plane(k), column(j), k * minor + j, mine).start()

    def multiply(k):
        x = plane(k)
        for j in range(minor):
            for t in range(1, m):
                copy = o_copy(t, x, column(j), k * minor + j, cols(lax.rem(core - t + m, m)))
                if j == 0:

                    @pl.when(k > 0)
                    def _():
                        copy.wait_recv()
                else:
                    copy.wait_recv()
        deep = pl.ds(pl.multiple_of(x * chunk, 128), chunk)

        def columns(c):
            at = pl.ds(pl.multiple_of(c * lanes, lanes), lanes)
            for i in range(2):
                acc[i, :, at] += jnp.dot(feats[i, :, deep], full[x, :, at], preferred_element_type=jnp.float32)

        each(0, width // lanes, columns)

    share(0)
    for copy in fetch:
        copy.wait()

    def steps(k):
        share(k)
        multiply(k - 1)

    each(1, major, steps)
    multiply(major - 1)
    first_embed[...] = acc[0].astype(first_embed.dtype)
    second_embed[...] = acc[1].astype(second_embed.dtype)

    def settle(k):
        for j in range(minor):
            for t in range(1, m):
                copy = o_copy(t, plane(k), column(j), k * minor + j, mine)
                if j == 0:

                    @pl.when(k > 0)
                    def _():
                        copy.wait_send()
                else:
                    copy.wait_send()
            if j > 0:
                p_copy(k, j, plane(k), b).wait_send()

    each(0, major, settle)
    each(1, major, lambda k: z_copy(k, a).wait_send())

    def questions(k):
        copy = q_copy(k, lax.rem(me - k + n, n))
        copy.wait_recv()
        copy.wait_send()

    each(1, n, questions)


def exchange_part(n, m, wanted, first_embed, second_embed, live, scale, got, out, s_all,
                  masked, rows, gram, away, landed, half, plane, line, lined, last, sums, s_core, rs, rr, os, orr, ps, pr, zs, zr, fs, fr, cs, cr, ss, sr):
    me, core = lax.axis_index("inner"), lax.axis_index("outer")
    minor = minor_size(n)
    major = n // minor
    a, b = me // minor, lax.rem(me, minor)
    part = out.shape[1] // m

    def cols(t):
        return pl.ds(pl.multiple_of(t * part, 128), part)

    mine = cols(core)
    tiles, width = second_embed.shape
    share, capacity = out.shape[0], rows.shape[1]
    lanes = min(width, 256)

    def o_copy(t):
        peer = lax.rem(core + t, m)
        return remote(away.at[:, cols(peer)], landed.at[t], (os, orr), t, {"outer": peer})

    def c_copy(t, index):
        return remote(sums, s_core.at[index], (cs, cr), t, {"outer": lax.rem(core + t, m)})

    def r_copy(k, index):
        peer = lax.rem(me + k, n)
        return remote(rows.at[peer], got.at[index], (rs, rr), k, {"inner": peer})

    def p_copy(j):
        other = lax.rem(b + j, minor)
        return remote(half.at[:, other], plane.at[j], (ps, pr), j, {"inner": a * minor + other})

    def z_copy(k):
        other = lax.rem(a + k, major)
        return remote(lined.at[other], last.at[k], (zs, zr), k, {"inner": other * minor + b})

    def s_copy(k, index):
        return remote(s_core, s_all.at[index], (ss, sr), k, {"inner": lax.rem(me + k, n)})

    def f_copy(t, lanes):
        return remote(out.at[:, lanes], out.at[:, lanes], (fs, fr), t, {"outer": lax.rem(core + t, m)})

    def pick(j):
        asked = wanted[j]
        onehot = lax.broadcasted_iota(jnp.int32, (tiles, asked.shape[1]), 0) == asked
        onehot = jnp.where(onehot, 1.0, 0.0).astype(jnp.bfloat16)
        chosen = lax.dot_general(
            onehot, second_embed[...], (((0,), (0,)), ((), ())), preferred_element_type=jnp.float32
        )
        rows[j] = chosen[:capacity].astype(rows.dtype)

    def serve(i):
        k = lax.rem(i + n // 2 - 1, n - 1) + 1
        pick(lax.rem(me + k, n))
        r_copy(k, me).start()

    each(0, n - 1, serve)
    pick(me)
    got[me] = rows[me]
    kept = first_embed[...].astype(jnp.float32) * live[...]
    masked[...] = kept.astype(masked.dtype)
    sums[...] = jnp.sum(kept, axis=0, keepdims=True)
    for t in range(1, m):
        c_copy(t, core).start()
    ones = jnp.ones((tiles, 128), jnp.bfloat16)

    def make_gram(c):
        at = pl.ds(pl.multiple_of(c * lanes, lanes), lanes)
        left = masked[:, at]
        value = lax.dot_general(left, masked[...], (((0,), (0,)), ((), ())), preferred_element_type=jnp.float32)
        column = lax.dot_general(left, ones, (((0,), (0,)), ((), ())), preferred_element_type=jnp.float32)
        value = value - column[:, :1] * (sums[...] * scale[...])
        gram[at, :] = value
        away[at, :] = value.astype(away.dtype)

    each(0, width // lanes, make_gram)
    for t in range(1, m):
        o_copy(t).start()
    s_core[core] = sums[...]
    for t in range(1, m):
        c_copy(t, lax.rem(core - t + m, m)).wait_recv()
    s_all[me] = s_core[...]
    each(1, n, lambda k: s_copy(k, me).start())
    for t in range(1, m):
        o_copy(t).wait_recv()

    def over_cores(x, y):
        at = pl.ds(pl.multiple_of((x * minor + y) * share, share), share)
        value = gram[at, mine]
        for t in range(1, m):
            value = value + landed[t, at].astype(jnp.float32)
        return value

    def add_cores(i):
        x, y = i // minor, lax.rem(i, minor)
        half[x, y] = over_cores(x, y).astype(half.dtype)

    each(0, n, add_cores)
    for j in range(1, minor):
        p_copy(j).start()
    for j in range(1, minor):
        p_copy(j).wait_recv()

    def add_plane(x):
        value = over_cores(x, b)
        for j in range(1, minor):
            value = value + plane[j, x].astype(jnp.float32)
        line[x] = value
        lined[x] = value.astype(lined.dtype)

    each(0, major, add_plane)
    each(1, major, lambda k: z_copy(k).start())
    each(1, major, lambda k: z_copy(k).wait_recv())
    value = line[a]
    for k in range(1, major):
        value = value + last[k].astype(jnp.float32)
    out[:, mine] = value
    for t in range(1, m):
        f_copy(t, mine).start()
    each(1, n, lambda k: s_copy(k, lax.rem(me - k + n, n)).wait_recv())

    def settle(k):
        r_copy(k, lax.rem(me - k + n, n)).wait_recv()
        r_copy(k, me).wait_send()
        s_copy(k, me).wait_send()

    each(1, n, settle)
    for t in range(1, m):
        f_copy(t, cols(lax.rem(core - t + m, m))).wait_recv()
        f_copy(t, mine).wait_send()
        o_copy(t).wait_send()
        c_copy(t, core).wait_send()
    for j in range(1, minor):
        p_copy(j).wait_send()
    each(1, major, lambda k: z_copy(k).wait_send())


def step_kernel(n, m, w, ask, first, second, live, scale, first_embed, got_rows, out, s_all, wanted, second_embed, *rest):
    gather_part(n, m, w, ask, first, second, wanted, first_embed, second_embed, *rest[:12])
    exchange_part(n, m, wanted, first_embed, second_embed, live, scale, got_rows, out, s_all, *rest[12:])


def step(expander, asked, first, second, live, scale, capacity, n, m):
    depth, width = expander.shape
    rows, channels = first.shape
    share, part = width // n, width // m
    minor = minor_size(n)
    major = n // minor
    dma = pltpu.SemaphoreType.DMA
    vmem = pl.BlockSpec(memory_space=pltpu.VMEM)
    anywhere = pl.BlockSpec(memory_space=pl.ANY)
    bf16, f32 = jnp.bfloat16, jnp.float32
    return pl.pallas_call(
        functools.partial(step_kernel, n, m),
        out_shape=(
            jax.ShapeDtypeStruct((rows, width), bf16),
            jax.ShapeDtypeStruct((n, capacity, width), bf16),
            jax.ShapeDtypeStruct((share, width), f32),
            jax.ShapeDtypeStruct((n, m, 1, width), f32),
        ),
        in_specs=[vmem, vmem, anywhere, anywhere, vmem, vmem],
        out_specs=(vmem,) * 4,
        scratch_shapes=[
            pltpu.VMEM(asked.shape, asked.dtype),
            pltpu.VMEM((rows, width), bf16),
            pltpu.VMEM((major, minor * depth, width), bf16),
            pltpu.VMEM((2, rows, channels), bf16),
            pltpu.VMEM((2, rows, width), f32),
        ]
        + [dma((size,)) for size in (major, n, m * n, n) for _ in range(2)]
        + [dma((2,))]
        + [
            pltpu.VMEM((rows, width), bf16),
            pltpu.VMEM((n, capacity, width), bf16),
            pltpu.VMEM((width, width), f32),
            pltpu.VMEM((width, width), bf16),
            pltpu.VMEM((m, width, part), bf16),
            pltpu.VMEM((major, minor, share, part), bf16),
            pltpu.VMEM((minor, major, share, part), bf16),
            pltpu.VMEM((major, share, part), f32),
            pltpu.VMEM((major, share, part), bf16),
            pltpu.VMEM((major, share, part), bf16),
            pltpu.VMEM((1, width), f32),
            pltpu.VMEM((m, 1, width), f32),
        ]
        + [dma((size,)) for size in (n, m, minor, major, m, m, n) for _ in range(2)],
        compiler_params=pltpu.CompilerParams(collective_id=0, has_side_effects=True, vmem_limit_bytes=48 << 20),
        name="step",
    )(expander, asked, first, second, live, scale)


def shards(feats_first, feats_second, expander, tile_count, match_dev, match_tile):
    first_rows = feats_first[0]
    second_rows = feats_second[0]
    tile_rows = first_rows.shape[0]
    expand_width = expander.shape[1]
    group_size = lax.axis_size("inner")
    capacity = -(-max(2, 3 * tile_rows // group_size) // 16) * 16
    slots = group_size * capacity
    inner_pos = lax.axis_index("inner")
    outer_pos = lax.axis_index("outer")
    target_dev = match_dev[0, :, 0]
    target_tile = match_tile[0]
    row_index = jnp.arange(tile_rows, dtype=jnp.int32)
    same = (target_dev[:, None] == target_dev[None, :]) & (row_index[None, :] < row_index[:, None])
    slot_pos = jnp.sum(same.astype(jnp.int32), axis=1)
    slot = target_dev * capacity + slot_pos
    chosen = slot[:, None] == jnp.arange(slots, dtype=jnp.int32)[None, :]
    padded = -(-capacity // 128) * 128
    asked = jnp.sum(jnp.where(chosen, target_tile[:, None], 0), axis=0).reshape(group_size, 1, capacity)
    asked = jnp.pad(asked, ((0, 0), (0, 0), (0, padded - capacity)))
    counts = lax.dynamic_index_in_dim(tile_count, outer_pos, 0, keepdims=False)
    own_count = lax.dynamic_index_in_dim(counts, inner_pos, 0, keepdims=False)
    live = row_index < own_count
    first_embed, recv_rows, gram_share, all_sums = step(
        expander,
        asked,
        first_rows,
        second_rows,
        live.astype(jnp.float32)[:, None],
        jnp.full((1, expand_width), 1.0 / own_count.astype(jnp.float32)),
        capacity,
        group_size,
        lax.axis_size("outer"),
    )
    recv_rows = recv_rows.reshape(slots, expand_width)
    partner = jnp.dot(chosen.astype(jnp.bfloat16), recv_rows, preferred_element_type=jnp.float32)
    dest_count = jnp.sum(
        jnp.where(target_dev[:, None] == jnp.arange(group_size, dtype=jnp.int32)[None, :], counts[None, :], 0), axis=1
    )
    valid = live & (target_tile < dest_count)
    diff = first_embed.astype(jnp.float32) - partner
    invariance = jnp.where(valid, jnp.mean(diff * diff, axis=-1), jnp.float32(0.0))
    total = jnp.sum(tile_count).astype(jnp.float32)
    share_rows = expand_width // group_size
    all_sums = all_sums.reshape(-1, expand_width)
    column_total = jnp.sum(all_sums, axis=0)
    own_part = lax.dynamic_slice_in_dim(all_sums, inner_pos * share_rows, share_rows, 1)
    own_sums = jnp.sum(own_part, axis=0)
    weights = 1.0 / tile_count.T.reshape(-1).astype(jnp.float32)
    between = lax.dot_general(
        own_part * weights[:, None], all_sums, (((0,), (0,)), ((), ())), precision=lax.Precision.HIGHEST
    )
    covariance = (gram_share + between - own_sums[:, None] * column_total[None, :] / total) / (total - 1.0)
    return (covariance, invariance[None, :])


def solution(mesh):
    return jax.shard_map(
        shards,
        mesh=mesh,
        in_specs=(
            P("outer", "inner", None),
            P("outer", "inner", None),
            P("inner", None),
            P(),
            P("outer", "inner", None),
            P("outer", "inner"),
        ),
        out_specs=(P("inner", None), P("outer", "inner")),
        check_vma=False,
    )
```
